512 devices in a mesh: mode: 16 (over y, core), cell: 32 (over z, x).
Axes of the slice: x: 4, y: 8, z: 8, core: 2. Of those that a mesh axis runs over, the one named last changes fastest.
Arguments:
- initial: float32 [1536, 64, 2048], P('mode', 'cell'), may hold values from -6 to 6
- scatter_matrix: bfloat16 [1536, 1536], replicated, may hold values from -0.15625 to 0.15625
- speed_x: float32 [1536], P('mode'), may hold values from -1 to 1
- speed_y: float32 [1536], P('mode'), may hold values from -1 to 1
- relaxation: float32 [1536], P('mode'), may hold values from 0.5 to 4
- emission: float32 [1536], P('mode'), may hold values from -4 to 4
- heater: int32 [64, 2048], P('cell'), may hold values 0 or 1
Outputs:
- distribution: float32 [1536, 64, 2048], P('mode', 'cell')
The draws below stay inside these ranges and needn't reach their ends.
All inputs are finite; a program needn't handle non-finite values. No bound on the sum of `heater` on one device may be relied on, other than what follows from the above.
Results may differ from the reference program's by a relative error of at most 0.0026.
Values may be sent and summed in bfloat16 or wider, within the bound.
No kernel may reach another device: no remote copies, remote signals or barrier semaphores. Data moves between devices by JAX's collectives and lax.ppermute only.
A program may use at most 64 MiB of HBM per device.

```python
import math
import jax
import jax.numpy as jnp
from jax import lax

M = 1536
NY = 2048
ITERS = 2
NX = 64


def place_ends(entries, stream_key, low, top_value):
    index_at = [jax.random.randint(jax.random.fold_in(stream_key, axis), (), 0, length) for axis, length in enumerate(entries.shape)]
    widest = entries.shape.index(max(entries.shape))
    next_to = index_at[:widest] + [(index_at[widest] + 1) % entries.shape[widest]] + index_at[widest + 1:]
    return entries.at[tuple(index_at)].set(low).at[tuple(next_to)].set(top_value)


def steps_of(key, shape, split, low, high):
    gain, own = 1.0, jax.random.fold_in(key, 6)
    for axis_at, parts in split:
        heights = jnp.exp(jax.random.uniform(jax.random.fold_in(own, axis_at), (parts,), jnp.float32, low / len(split), high / len(split)))
        gain = gain * jnp.repeat(heights, shape[axis_at] // parts).reshape([-1 if axis == axis_at else 1 for axis in range(len(shape))])
    return gain


def gaussian(rng, dims, width, limit, shards=(), held_as=jnp.bfloat16):
    result = width * jax.random.normal(rng, dims, jnp.float32)
    if shards:
        result = result * steps_of(rng, dims, shards, -0.22, 0.18)
    return jnp.clip(result, -limit, limit).astype(held_as)


def setup_inputs(seed: int = 0) -> dict:
    streams_of = jax.random.split(jax.random.key(seed), 8)
    initial = gaussian(streams_of[0], (M, NX, NY), 1.0, 6.0, ((0, 16), (1, 32)), jnp.float32)
    scatter_matrix = gaussian(streams_of[1], (M, M), M ** -0.5, 0.15625)
    speed_x = jnp.clip(jax.random.uniform(streams_of[2], (M,), jnp.float32, -1.0, 1.0) * steps_of(streams_of[2], (M,), ((0, 16),), -0.4, 0.0), -1.0, 1.0)
    speed_y = jnp.clip(jax.random.uniform(streams_of[3], (M,), jnp.float32, -1.0, 1.0) * steps_of(streams_of[3], (M,), ((0, 16),), -0.4, 0.0), -1.0, 1.0)
    relaxation = jnp.clip(jnp.exp(math.log(4.0) - 2.0794415 * jax.random.uniform(streams_of[4], (M,), jnp.float32) ** steps_of(streams_of[4], (M,), ((0, 16),), -0.2, 0.2)), 0.5, 4.0)
    emission = gaussian(streams_of[5], (M,), 1.0, 4.0, ((0, 16),), jnp.float32)
    heater = place_ends((jax.random.randint(streams_of[6], (NX, NY), 0, 4) < 1).astype(jnp.int32), jax.random.fold_in(streams_of[6], 1), 0, 1)
    return dict(initial=initial, scatter_matrix=scatter_matrix, speed_x=speed_x, speed_y=speed_y, relaxation=relaxation, emission=emission, heater=heater)


def stream_y(field, speed_y):
    padded = jnp.pad(field, ((0, 0), (0, 0), (1, 1)))
    return jnp.where(speed_y[:, None, None] > 0, padded[:, :, :-2], padded[:, :, 2:])


def reference(initial, scatter_matrix, speed_x, speed_y, relaxation, emission, heater):
    rate_x = jnp.abs(speed_x)[:, None, None]
    rate_y = jnp.abs(speed_y)[:, None, None]
    denominator = relaxation[:, None, None] + rate_x + rate_y
    source = heater.astype(jnp.float32)[None, :, :] * emission[:, None, None]
    field = initial
    for step in range(ITERS):
        narrow = field.astype(jnp.bfloat16)

        def one_column(index_row):
            slab = lax.dynamic_index_in_dim(narrow, index_row, 1, False)
            return jnp.dot(scatter_matrix, slab, preferred_element_type=jnp.float32)

        columns = lax.map(one_column, jnp.arange(NX, dtype=jnp.int32))
        scattered = jnp.transpose(columns, (1, 0, 2))
        padded = jnp.pad(field, ((0, 0), (1, 1), (0, 0)))
        from_x = jnp.where(speed_x[:, None, None] > 0, padded[:, :-2, :], padded[:, 2:, :])
        from_y = stream_y(field, speed_y)
        field = (rate_x * from_x + rate_y * from_y + scattered + source) / denominator
    return field
```

```python
import jax
import jax.numpy as jnp
from jax import lax
from jax.sharding import PartitionSpec as P

F32 = jnp.float32
BF16 = jnp.bfloat16


def shift_pairs(count, step):
    return [(i, i + step) for i in range(count) if 0 <= i + step < count]


def swap(values, axis):
    onward, back = values
    count = lax.axis_size(axis)
    return (
        lax.ppermute(onward, axis, shift_pairs(count, 1)),
        lax.ppermute(back, axis, shift_pairs(count, -1)),
    )


def shards(initial, scatter_matrix, speed_x, speed_y, relaxation, emission, heater):
    modes, cols, length = initial.shape
    groups = lax.axis_size("mode")
    span = length // groups
    cells = cols * span
    total = modes * groups

    packed = initial.astype(BF16).reshape(modes, cols, groups, span)
    packed = packed.transpose(2, 0, 1, 3).reshape(groups, modes, cells)
    own = lax.all_to_all(packed, "mode", 0, 0, tiled=True).reshape(total, cells)

    params = lax.all_gather(
        jnp.stack([speed_x, speed_y, relaxation, emission]), "mode", axis=1, tiled=True
    )
    sx, sy, rel, emit = (params[k][:, None] for k in range(4))
    inverse = 1.0 / (rel + jnp.abs(sx) + jnp.abs(sy))
    x_up, x_down = jnp.maximum(sx, 0.0) * inverse, jnp.maximum(-sx, 0.0) * inverse
    y_up, y_down = jnp.maximum(sy, 0.0) * inverse, jnp.maximum(-sy, 0.0) * inverse
    heat = lax.dynamic_slice_in_dim(heater, lax.axis_index("mode") * span, span, axis=1)
    source = heat.astype(F32).reshape(1, cells) * (emit * inverse)

    def ends(field):
        first = jnp.concatenate([field[:, c * span : c * span + 1] for c in range(cols)], axis=1)
        last = jnp.concatenate([field[:, (c + 1) * span - 1 : (c + 1) * span] for c in range(cols)], axis=1)
        return first.T, last.T

    def along_y(field, before, after):
        before, after = before.T, after.T
        up, down = [], []
        for c in range(cols):
            part = field[:, c * span : (c + 1) * span]
            up += [before[:, c : c + 1], part[:, :-1]]
            down += [part[:, 1:], after[:, c : c + 1]]
        return (
            y_up * jnp.concatenate(up, axis=1).astype(F32)
            + y_down * jnp.concatenate(down, axis=1).astype(F32)
        )

    def scatter(field):
        return inverse * jnp.dot(scatter_matrix, field, preferred_element_type=F32)

    def inner_x(field):
        zero = jnp.zeros((total, span), F32)
        wide = field.astype(F32)
        return x_up * jnp.concatenate([zero, wide[:, :-span]], axis=1) + x_down * jnp.concatenate(
            [wide[:, span:], zero], axis=1
        )

    def outer_x(left, right):
        zero = jnp.zeros((total, cells - 2 * span), F32)
        return jnp.concatenate(
            [x_up * left.astype(F32), zero, x_down * right.astype(F32)], axis=1
        )

    x_before, x_after = swap((own[:, -span:], own[:, :span]), "cell")
    first, last = ends(own)
    y_before, y_after = swap((last, first), "mode")
    partial = scatter(own) + source + inner_x(own) + along_y(own, y_before, y_after)
    sent = partial.astype(BF16)
    x_before_2, x_after_2 = swap((sent[:, -span:], sent[:, :span]), "cell")
    field = (partial + outer_x(x_before, x_after)).astype(BF16)

    first, last = ends(field)
    y_before, y_after = swap((last, first), "mode")
    result = (
        scatter(field)
        + source
        + inner_x(field)
        + along_y(field, y_before, y_after)
        + outer_x(x_before_2, x_after_2)
    )
    result = result.astype(BF16).reshape(groups, modes, cells)
    out = lax.all_to_all(result, "mode", 0, 0, tiled=True)
    out = out.reshape(groups, modes, cols, span).transpose(1, 2, 0, 3)
    return out.reshape(modes, cols, length).astype(F32)


def solution(mesh):
    return jax.shard_map(
        shards,
        mesh=mesh,
        in_specs=(
            P("mode", "cell", None),
            P(),
            P("mode"),
            P("mode"),
            P("mode"),
            P("mode"),
            P("cell", None),
        ),
        out_specs=P("mode", "cell", None),
        check_vma=False,
    )
```

```python
import jax
import jax.numpy as jnp
from jax import lax
from jax.sharding import PartitionSpec as P

F32 = jnp.float32
BF16 = jnp.bfloat16
LANES = 128


def shift_pairs(count, step):
    return [(i, i + step) for i in range(count) if 0 <= i + step < count]


def swap(onward, back):
    count = lax.axis_size("cell")
    return (
        lax.ppermute(onward, "cell", shift_pairs(count, 1)),
        lax.ppermute(back, "cell", shift_pairs(count, -1)),
    )


def two_parts(vectors):
    high = lax.reduce_precision(vectors, 8, 7)
    return high.astype(BF16), (vectors - high).astype(BF16)


def shards(initial, scatter_matrix, speed_x, speed_y, relaxation, emission, heater):
    modes, cols, length = initial.shape
    groups = lax.axis_size("mode")
    span = length // groups
    cells = cols * span
    total = modes * groups

    packed = initial.astype(BF16).reshape(modes, cols, groups, span).transpose(2, 0, 1, 3)
    low = jnp.pad(packed[:-1, :, :, span - 2 :], ((1, 0), (0, 0), (0, 0), (0, 0)))
    high = jnp.pad(packed[1:, :, :, :2], ((0, 1), (0, 0), (0, 0), (0, 0)))
    edges = jnp.concatenate([low, high], axis=3).transpose(0, 2, 3, 1)
    edges = edges.reshape(groups, 4 * cols, modes)
    inverse = 1.0 / (relaxation + jnp.abs(speed_x) + jnp.abs(speed_y))
    vectors = jnp.stack([speed_x * inverse, speed_y * inverse, inverse, emission * inverse])
    vectors = jnp.concatenate(two_parts(vectors), axis=0)
    vectors = jnp.broadcast_to(vectors[None], (groups, 8, modes))
    extra = jnp.concatenate([edges, vectors], axis=1)
    extra = jnp.pad(extra, ((0, 0), (0, 0), (0, LANES - modes))).reshape(groups, 8, 2 * LANES)
    packed = packed.reshape(groups, modes, cells)
    received = lax.all_to_all(
        jnp.concatenate([packed, extra], axis=1), "mode", 0, 0, tiled=True
    )

    own = received[:, :modes].reshape(total, cols, span).transpose(1, 2, 0)
    extra = received[:, modes:].reshape(groups, 16, LANES)[:, :, :modes]
    extra = extra.transpose(1, 0, 2).reshape(16, total)
    edges = extra[:8].reshape(cols, 4, total)
    own = jnp.concatenate([edges[:, :2], own, edges[:, 2:]], axis=1)
    vectors = extra[8:12].astype(F32) + extra[12:].astype(F32)
    x_up, x_down = jnp.maximum(vectors[0], 0.0), jnp.maximum(-vectors[0], 0.0)
    y_up, y_down = jnp.maximum(vectors[1], 0.0), jnp.maximum(-vectors[1], 0.0)
    inverse, emit = vectors[2], vectors[3]
    heat = jnp.pad(heater.astype(F32), ((0, 0), (1, 1)))
    heat = lax.dynamic_slice_in_dim(heat, lax.axis_index("mode") * span, span + 2, axis=1)
    heat = heat[:, :, None]

    def scatter(field):
        return inverse * lax.dot_general(
            field, scatter_matrix, (((2,), (1,)), ((), ())), preferred_element_type=F32
        )

    def local(scattered, field, heat):
        wide = field.astype(F32)
        inner = wide[:, 1:-1]
        first = x_down * inner[1]
        second = x_up * inner[0]
        return (
            scattered
            + heat * emit
            + y_up * wide[:, :-2]
            + y_down * wide[:, 2:]
            + jnp.stack([first, second])
        )

    left, right = swap(own[1, 1:-1], own[0, 1:-1])
    partial = local(scatter(own[:, 1:-1]), own, heat)
    partial = lax.optimization_barrier(partial)
    sent = partial[:, 1:-1].astype(BF16)
    left_2, right_2 = swap(sent[1], sent[0])
    field = partial + jnp.stack([x_up * left.astype(F32), x_down * right.astype(F32)])

    result = local(scatter(field[:, 1:-1].astype(BF16)), field, heat[:, 1:-1])
    result = lax.optimization_barrier(result)
    result = result + jnp.stack([x_up * left_2.astype(F32), x_down * right_2.astype(F32)])
    result = result.astype(BF16).transpose(2, 0, 1).reshape(groups, modes, cells)
    out = lax.all_to_all(result, "mode", 0, 0, tiled=True)
    out = out.reshape(groups, modes, cols, span).transpose(1, 2, 0, 3)
    return out.reshape(modes, cols, length).astype(F32)


def solution(mesh):
    return jax.shard_map(
        shards,
        mesh=mesh,
        in_specs=(
            P("mode", "cell", None),
            P(),
            P("mode"),
            P("mode"),
            P("mode"),
            P("mode"),
            P("cell", None),
        ),
        out_specs=P("mode", "cell", None),
        check_vma=False,
    )
```

```python
import jax
import jax.numpy as jnp
from jax import lax
from jax.experimental import pallas as pl
from jax.experimental.pallas import tpu as pltpu
from jax.sharding import PartitionSpec as P

F32 = jnp.float32
BF16 = jnp.bfloat16
SIDE = 8
TILE = 256
MIB = 1024 * 1024


def shift_pairs(count, step):
    return [(i, i + step) for i in range(count) if 0 <= i + step < count]


def swap(onward, back):
    count = lax.axis_size("cell")
    return (
        lax.ppermute(onward, "cell", shift_pairs(count, 1)),
        lax.ppermute(back, "cell", shift_pairs(count, -1)),
    )


IN_VMEM = pl.BlockSpec(memory_space=pltpu.VMEM)
IN_HBM = pl.BlockSpec(memory_space=pltpu.HBM)


def params(limit):
    return pltpu.CompilerParams(vmem_limit_bytes=limit * MIB)


def iota(shape, axis):
    return lax.broadcasted_iota(jnp.int32, shape, axis)


def pack_body(speed_x_in, speed_y_in, relaxation_in, emission_in, initial_in, packed, *scratch):
    arrived = scratch[-1]
    sources = (speed_x_in, speed_y_in, relaxation_in, emission_in, initial_in)
    copies = [
        pltpu.make_async_copy(source, place, arrived.at[k])
        for k, (source, place) in enumerate(zip(sources, scratch[:-1]))
    ]
    for copy in copies:
        copy.start()
    for copy in copies:
        copy.wait()
    speed_x, speed_y, relaxation, emission, initial = scratch[:-1]
    groups, height, cells = packed.shape
    modes, span = height - SIDE, cells // 2
    sx, sy = speed_x[...], speed_y[...]
    inverse = 1.0 / (relaxation[...] + jnp.abs(sx) + jnp.abs(sy))
    vectors = jnp.concatenate([sx * inverse, sy * inverse, inverse, emission[...] * inverse], axis=0)
    high = vectors.astype(BF16).astype(F32)
    vectors = jnp.concatenate([high, vectors - high], axis=0)
    vectors = jnp.concatenate([vectors, jnp.zeros((SIDE, span - modes), F32)], axis=1)
    row, lane = iota((SIDE, cells), 0), iota((SIDE, cells), 1)
    pair, odd = row // 2, row % 2
    column = ((pair == 1) | (pair == 2)).astype(jnp.int32)
    after = (pair == 0) | (pair == 2)
    pick = lane == column * span + jnp.where(after, odd, span - 2 + odd)
    pick = jnp.where(pick, 1.0, 0.0).astype(BF16)
    is_after = ((iota((SIDE, span), 0) // 2) % 2) == 0
    ends = []
    for group in range(groups):
        at = pl.ds(group * span, span)
        block = jnp.concatenate([initial[:, c, at] for c in range(2)], axis=1).astype(BF16)
        packed[group, :modes, :] = block
        block = jnp.concatenate([block, jnp.zeros((span - modes, cells), BF16)], axis=0)
        ends.append(
            lax.dot_general(pick, block, (((1,), (1,)), ((), ())), preferred_element_type=F32)
        )
    none = jnp.zeros((SIDE, span), F32)
    for group in range(groups):
        after = ends[group + 1] if group + 1 < groups else none
        before = ends[group - 1] if group else none
        edge = jnp.where(is_after, after, before)
        packed[group, modes:, :] = jnp.concatenate([edge, vectors], axis=1).astype(BF16)


def pack(initial, vectors, groups):
    modes, cols, length = initial.shape
    shape = (groups, modes + SIDE, cols * length // groups)
    return pl.pallas_call(
        pack_body,
        in_specs=[IN_HBM] * 5,
        out_specs=IN_VMEM,
        scratch_shapes=[pltpu.VMEM((1, modes), F32)] * 4
        + [pltpu.VMEM(initial.shape, F32), pltpu.SemaphoreType.DMA((5,))],
        out_shape=jax.ShapeDtypeStruct(shape, BF16),
        compiler_params=params(32),
        cost_estimate=pl.CostEstimate(flops=10**7, bytes_accessed=3 * MIB, transcendentals=0),
        name="pack",
    )(*[v[None] for v in vectors], initial)


def unpack_body(received, own_0, own_1, coef):
    groups, height, cells = received.shape
    modes, span = height - SIDE, cells // 2
    unit = jnp.where(iota((span, span), 0) == iota((span, span), 1), 1.0, 0.0).astype(BF16)
    together = 4
    wide = together * modes
    for first in range(0, groups, together):
        lanes = pl.ds(first // together * wide, wide)
        members = range(first, first + together)
        edge = jnp.concatenate([received[j, modes:, :modes] for j in members], axis=1).astype(F32)
        vector = jnp.concatenate(
            [received[j, modes:, span : span + modes] for j in members], axis=1
        ).astype(F32)
        coef[:, lanes] = vector + pltpu.roll(vector, 4, 0)
        for c, out in ((0, own_0), (1, own_1)):
            block = jnp.concatenate(
                [received[j, :modes, c * span : (c + 1) * span] for j in members], axis=0
            )
            turned = lax.dot_general(
                unit, block, (((1,), (1,)), ((), ())), preferred_element_type=F32
            )
            ends = edge if c == 0 else pltpu.roll(edge, 4, 0)
            out[:, lanes] = jnp.concatenate([turned, ends], axis=0).astype(BF16)


def unpack(received):
    groups, height, cells = received.shape
    total, rows = groups * (height - SIDE), cells // 2 + SIDE
    return pl.pallas_call(
        unpack_body,
        out_shape=[jax.ShapeDtypeStruct((rows, total), BF16)] * 2
        + [jax.ShapeDtypeStruct((SIDE, total), F32)],
        compiler_params=params(32),
        cost_estimate=pl.CostEstimate(flops=10**7, bytes_accessed=3 * MIB, transcendentals=0),
        name="unpack",
    )(received)


def scatter(matrix, values):
    return lax.dot_general(
        values, matrix, (((1,), (0,)), ((), ())), preferred_element_type=F32
    )


def local_terms(scattered, mine, other, x_rate, coef, heat):
    rows, kept = mine.shape[0], scattered.shape[0]
    y_rate, inverse, emit = (coef[k : k + 1, :] for k in (1, 2, 3))
    return (
        scattered * inverse
        + heat * emit
        + jnp.maximum(y_rate, 0.0) * pltpu.roll(mine, 1, 0)[:kept]
        + jnp.maximum(-y_rate, 0.0) * pltpu.roll(mine, rows - 1, 0)[:kept]
        + x_rate * other[:kept]
    )


def first_body(own_0, own_1, matrix, coef, heat, part_0, part_1, sent_0, sent_1, both):
    rows, total = own_0.shape
    both[:rows, :] = own_0[...].astype(F32).astype(BF16)
    both[rows:, :] = own_1[...].astype(F32).astype(BF16)
    for first in range(0, total, TILE):
        at = pl.ds(first, TILE)
        x_rate = coef[0:1, at]
        wide_0, wide_1 = own_0[:, at].astype(F32), own_1[:, at].astype(F32)
        scattered = scatter(matrix[:, at], both[...])
        value = local_terms(
            scattered[:rows], wide_0, wide_1, jnp.maximum(-x_rate, 0.0), coef[:, at], heat[0]
        )
        part_0[:, at] = value
        sent_0[:, at] = value.astype(BF16)
        value = local_terms(
            scattered[rows:], wide_1, wide_0, jnp.maximum(x_rate, 0.0), coef[:, at], heat[1]
        )
        part_1[:, at] = value
        sent_1[:, at] = value.astype(BF16)


def first_step(own_0, own_1, matrix, coef, heat):
    rows, total = own_0.shape
    return pl.pallas_call(
        first_body,
        in_specs=[IN_VMEM] * 5,
        out_specs=[IN_VMEM] * 4,
        out_shape=[jax.ShapeDtypeStruct((rows, total), F32)] * 2
        + [jax.ShapeDtypeStruct((rows, total), BF16)] * 2,
        scratch_shapes=[pltpu.VMEM((2 * rows, total), BF16)],
        compiler_params=params(24),
        cost_estimate=pl.CostEstimate(
            flops=4 * rows * total * total, bytes_accessed=8 * MIB, transcendentals=0
        ),
        name="first_step",
    )(own_0, own_1, matrix, coef, heat)


def second_body(part_0, part_1, left, right, matrix, coef, heat, base_0, base_1, field, narrow):
    span, total = base_0.shape
    x_rate = coef[0:1, :]
    field[0] = part_0[...] + jnp.maximum(x_rate, 0.0) * left[...].astype(F32)
    field[1] = part_1[...] + jnp.maximum(-x_rate, 0.0) * right[...].astype(F32)
    for c in range(2):
        narrow[c * span : (c + 1) * span, :] = field[c, :span, :].astype(BF16)
    for first in range(0, total, TILE):
        at = pl.ds(first, TILE)
        x_rate = coef[0:1, at]
        scattered = scatter(matrix[:, at], narrow[...])
        mine_0, mine_1 = field[0, :, at], field[1, :, at]
        base_0[:, at] = local_terms(
            scattered[:span], mine_0, mine_1, jnp.maximum(-x_rate, 0.0), coef[:, at], heat[0, :span]
        )
        base_1[:, at] = local_terms(
            scattered[span:], mine_1, mine_0, jnp.maximum(x_rate, 0.0), coef[:, at], heat[1, :span]
        )


def second_step(part_0, part_1, left, right, matrix, coef, heat):
    rows, total = part_0.shape
    span = rows - SIDE
    return pl.pallas_call(
        second_body,
        in_specs=[IN_VMEM] * 7,
        out_specs=[IN_VMEM] * 2,
        out_shape=[jax.ShapeDtypeStruct((span, total), F32)] * 2,
        scratch_shapes=[pltpu.VMEM((2, rows, total), F32), pltpu.VMEM((2 * span, total), BF16)],
        compiler_params=params(24),
        cost_estimate=pl.CostEstimate(
            flops=4 * rows * total * total, bytes_accessed=8 * MIB, transcendentals=0
        ),
        name="second_step",
    )(part_0, part_1, left, right, matrix, coef, heat)


def finish_body(base_0, base_1, left, right, coef, result):
    groups, modes, cells = result.shape
    span = cells // 2
    unit = jnp.where(iota((span, span), 0) == iota((span, span), 1), 1.0, 0.0).astype(BF16)
    together = 4
    wide = together * modes
    for first in range(0, groups, together):
        lanes = pl.ds(first // together * wide, wide)
        x_rate = coef[0:1, lanes]
        for c, base, outer, rate in (
            (0, base_0, left, jnp.maximum(x_rate, 0.0)),
            (1, base_1, right, jnp.maximum(-x_rate, 0.0)),
        ):
            value = base[:, lanes] + rate * outer[:span, lanes].astype(F32)
            turned = lax.dot_general(
                value.astype(BF16), unit, (((0,), (0,)), ((), ())), preferred_element_type=F32
            ).astype(BF16)
            for k in range(together):
                result[first + k, :, c * span : (c + 1) * span] = turned[k * modes : (k + 1) * modes]


def finish(base_0, base_1, left, right, coef, groups):
    span, total = base_0.shape
    return pl.pallas_call(
        finish_body,
        out_shape=jax.ShapeDtypeStruct((groups, total // groups, 2 * span), BF16),
        compiler_params=params(32),
        cost_estimate=pl.CostEstimate(flops=10**7, bytes_accessed=3 * MIB, transcendentals=0),
        name="finish",
    )(base_0, base_1, left, right, coef)


def shards(initial, scatter_matrix, speed_x, speed_y, relaxation, emission, heater):
    modes, cols, length = initial.shape
    groups = lax.axis_size("mode")
    span = length // groups

    turned = lax.optimization_barrier(scatter_matrix.T)
    packed = pack(initial, (speed_x, speed_y, relaxation, emission), groups)
    received = lax.all_to_all(packed, "mode", 0, 0, tiled=True)
    own_0, own_1, coef = unpack(received)

    heat = jnp.pad(heater.astype(F32), ((0, 0), (2, 2)))
    heat = lax.dynamic_slice_in_dim(heat, lax.axis_index("mode") * span, span + 4, axis=1)
    none = jnp.zeros((cols, 4), F32)
    heat = jnp.concatenate([heat[:, 2:], none, heat[:, :2]], axis=1)[:, :, None]

    left, right = swap(own_1, own_0)
    part_0, part_1, sent_0, sent_1 = first_step(own_0, own_1, turned, coef, heat)
    left_2, right_2 = swap(sent_1, sent_0)
    base_0, base_1 = second_step(part_0, part_1, left, right, turned, coef, heat)
    result = finish(base_0, base_1, left_2, right_2, coef, groups)

    out = lax.all_to_all(result, "mode", 0, 0, tiled=True)
    out = out.reshape(groups, modes, cols, span).transpose(1, 2, 0, 3)
    return out.reshape(modes, cols, length).astype(F32)


def solution(mesh):
    return jax.shard_map(
        shards,
        mesh=mesh,
        in_specs=(
            P("mode", "cell", None),
            P(),
            P("mode"),
            P("mode"),
            P("mode"),
            P("mode"),
            P("cell", None),
        ),
        out_specs=P("mode", "cell", None),
        check_vma=False,
    )
```

```python
import jax
import jax.numpy as jnp
from jax import lax
from jax.experimental import pallas as pl
from jax.experimental.pallas import tpu as pltpu
from jax.sharding import PartitionSpec as P

F32 = jnp.float32
BF16 = jnp.bfloat16
SIDE = 8
TILE = 256
MIB = 1024 * 1024
PIECES = 4
PACK_LIMIT = 62


def swap(to_first, to_second):
    count = lax.axis_size("cell")
    first = [(i, i ^ 1) for i in range(count)]
    second = [(i, i + 1 if i % 2 else i - 1) for i in range(count)]
    inside = lambda pairs: [(i, j) for i, j in pairs if 0 <= j < count]
    return (
        lax.ppermute(to_first, "cell", inside(first)),
        lax.ppermute(to_second, "cell", inside(second)),
    )


IN_VMEM = pl.BlockSpec(memory_space=pltpu.VMEM)
IN_HBM = pl.BlockSpec(memory_space=pltpu.HBM)


def params(limit):
    return pltpu.CompilerParams(vmem_limit_bytes=limit * MIB)


def one_hot(mask):
    return jnp.where(mask, 1.0, 0.0).astype(BF16)


def iota(shape, axis):
    return lax.broadcasted_iota(jnp.int32, shape, axis)


def pack_body(
    speed_x_in, speed_y_in, relaxation_in, emission_in, initial_in, packed,
    speed_x, speed_y, relaxation, emission, initial, arrived,
):
    groups, height, cells = packed.shape
    modes, span = height - SIDE, cells // 2
    per = groups // PIECES
    pairs = ((speed_x_in, speed_x), (speed_y_in, speed_y), (relaxation_in, relaxation), (emission_in, emission))
    small = [pltpu.make_async_copy(*pair, arrived.at[k]) for k, pair in enumerate(pairs)]
    large = []
    for k in range(PIECES):
        at = pl.ds(k * per * span, per * span)
        large.append(
            pltpu.make_async_copy(initial_in.at[:, :, at], initial.at[:, :, at], arrived.at[4 + k])
        )
    for copy in large[:1] + small + large[1:]:
        copy.start()
    wide = 2 * modes
    row, lane = iota((wide, wide), 0), iota((wide, wide), 1)
    apart = one_hot(lane == jnp.where(row < modes, 2 * row, 2 * (row - modes) + 1))
    row, lane = iota((per * span, groups * SIDE), 0), iota((per * span, groups * SIDE), 1)
    after = (lane // 2) % 2 == 0
    target = lane // SIDE * span + lane % 2 + jnp.where(after, span, -2) - row
    ends = jnp.zeros((wide, groups * SIDE), F32)
    for k in range(PIECES):
        large[k].wait()
        first = k * per * span
        both = [
            initial[:, :, pl.ds(first + g * span, span)].reshape(wide, span).astype(BF16)
            for g in range(per)
        ]
        both = jnp.concatenate(both, axis=1)
        ends += jnp.dot(both, one_hot(target == first), preferred_element_type=F32)
        both = jnp.dot(apart, both, preferred_element_type=F32).astype(BF16)
        for g in range(per):
            at = slice(g * span, (g + 1) * span)
            packed[k * per + g, :modes, :] = jnp.concatenate([both[:modes, at], both[modes:, at]], axis=1)
    ends = jnp.dot(apart, ends.astype(BF16), preferred_element_type=F32)
    ends = jnp.concatenate(
        [ends[:modes], jnp.zeros((span - modes, groups * SIDE), F32),
         ends[modes:], jnp.zeros((span - modes, groups * SIDE), F32)], axis=0
    ).T
    middle = (iota((groups * SIDE, span), 0) % SIDE) // 2
    ends = jnp.where((middle == 1) | (middle == 2), ends[:, span:], ends[:, :span])
    for copy in small:
        copy.wait()
    sx, sy = speed_x[...], speed_y[...]
    inverse = 1.0 / (relaxation[...] + jnp.abs(sx) + jnp.abs(sy))
    vectors = jnp.concatenate([sx * inverse, sy * inverse, inverse, emission[...] * inverse], axis=0)
    high = vectors.astype(BF16).astype(F32)
    vectors = jnp.concatenate([high, vectors - high], axis=0)
    vectors = jnp.concatenate([vectors, jnp.zeros((SIDE, span - modes), F32)], axis=1)
    for group in range(groups):
        edge = ends[group * SIDE : (group + 1) * SIDE]
        packed[group, modes:, :] = jnp.concatenate([edge, vectors], axis=1).astype(BF16)


def pack(initial, vectors, groups):
    modes, cols, length = initial.shape
    shape = (groups, modes + SIDE, cols * length // groups)
    return pl.pallas_call(
        pack_body,
        in_specs=[IN_HBM] * 5,
        out_specs=IN_VMEM,
        scratch_shapes=[pltpu.VMEM((1, modes), F32)] * 4
        + [pltpu.VMEM(initial.shape, F32), pltpu.SemaphoreType.DMA((4 + PIECES,))],
        out_shape=jax.ShapeDtypeStruct(shape, BF16),
        compiler_params=params(PACK_LIMIT),
        cost_estimate=pl.CostEstimate(flops=10**7, bytes_accessed=3 * MIB, transcendentals=0),
        name="pack",
    )(*[v[None] for v in vectors], initial)


def unpack_body(received, heater, own_0, own_1, coef, heat):
    groups, height, cells = received.shape
    modes, span = height - SIDE, cells // 2
    unit = one_hot(iota((span, span), 0) == iota((span, span), 1))
    me = lax.axis_index("mode")
    even = lax.axis_index("cell") % 2 == 0
    parts = []
    for k in (-1, 0, 1):
        there = me + k
        inside = ((there >= 0) & (there < groups)).astype(jnp.int32)
        at = pl.ds(pl.multiple_of(jnp.clip(there, 0, groups - 1) * span, span), span)
        parts.append(heater[:, at] * inside)
    near = jnp.concatenate(parts, axis=1).astype(F32)
    near = jnp.where(even, jnp.concatenate([near[1:], near[:1]], axis=0), near)
    near = jnp.concatenate([near, jnp.zeros((SIDE - 2, 3 * span), F32)], axis=0).astype(BF16)
    row, lane = iota((span + SIDE, 3 * span), 0), iota((span + SIDE, 3 * span), 1)
    pick = one_hot(lane == jnp.where(row < span + SIDE // 2, span + row, row - SIDE))
    heat[...] = lax.dot_general(pick, near, (((1,), (1,)), ((), ())), preferred_element_type=F32)
    together = 4
    wide = together * modes
    for first in range(0, groups, together):
        lanes = pl.ds(first // together * wide, wide)
        members = range(first, first + together)
        edge = jnp.concatenate([received[j, modes:, :modes] for j in members], axis=1).astype(F32)
        vector = jnp.concatenate(
            [received[j, modes:, span : span + modes] for j in members], axis=1
        ).astype(F32)
        vector = vector + pltpu.roll(vector, 4, 0)
        sign = jnp.where((iota((SIDE, wide), 0) == 0) & jnp.logical_not(even), -1.0, 1.0)
        coef[:, lanes] = vector * sign
        other = pltpu.roll(edge, 4, 0)
        for c, out in ((0, own_0), (1, own_1)):
            column = jnp.where(even, 1 - c, c)
            at = pl.ds(pl.multiple_of(column * span, span), span)
            block = jnp.concatenate([received[j, :modes, at] for j in members], axis=0)
            turned = lax.dot_general(
                unit, block, (((1,), (1,)), ((), ())), preferred_element_type=F32
            )
            ends = jnp.where(column == 0, edge, other)
            out[:, lanes] = jnp.concatenate([turned, ends], axis=0).astype(BF16)


def unpack(received, heater):
    groups, height, cells = received.shape
    total, rows = groups * (height - SIDE), cells // 2 + SIDE
    return pl.pallas_call(
        unpack_body,
        in_specs=[IN_VMEM] * 2,
        out_specs=[IN_VMEM] * 4,
        out_shape=[jax.ShapeDtypeStruct((rows, total), BF16)] * 2
        + [jax.ShapeDtypeStruct((SIDE, total), F32), jax.ShapeDtypeStruct((rows, SIDE), F32)],
        compiler_params=params(24),
        cost_estimate=pl.CostEstimate(flops=10**7, bytes_accessed=3 * MIB, transcendentals=0),
        name="unpack",
    )(received, heater)


def scatter(matrix, values):
    return lax.dot_general(
        values, matrix, (((1,), (1,)), ((), ())), preferred_element_type=F32
    )


def local_terms(scattered, mine, other, x_rate, coef, heat):
    rows, kept = mine.shape[0], scattered.shape[0]
    y_rate, inverse, emit = (coef[k : k + 1, :] for k in (1, 2, 3))
    return (
        scattered * inverse
        + heat * emit
        + jnp.maximum(y_rate, 0.0) * pltpu.roll(mine, 1, 0)[:kept]
        + jnp.maximum(-y_rate, 0.0) * pltpu.roll(mine, rows - 1, 0)[:kept]
        + x_rate * other[:kept]
    )


def first_body(own_0, own_1, matrix, coef, heat, part_0, part_1, sent_0, sent_1, both):
    rows, total = own_0.shape
    span = rows - SIDE
    both[:rows, :] = own_0[...].astype(F32).astype(BF16)
    both[rows:, :] = own_1[...].astype(F32).astype(BF16)
    for first in range(0, total, TILE):
        at = pl.ds(first, TILE)
        x_rate = coef[0:1, at]
        wide_0, wide_1 = own_0[:, at].astype(F32), own_1[:, at].astype(F32)
        scattered = scatter(matrix[at, :], both[...])
        value = local_terms(
            scattered[:rows], wide_0, wide_1, jnp.maximum(x_rate, 0.0), coef[:, at], heat[:, 0:1]
        )
        part_0[:, at] = value
        sent_0[:, at] = value[:span].astype(BF16)
        value = local_terms(
            scattered[rows:], wide_1, wide_0, jnp.maximum(-x_rate, 0.0), coef[:, at], heat[:, 1:2]
        )
        part_1[:, at] = value
        sent_1[:, at] = value[:span].astype(BF16)


def first_step(own_0, own_1, matrix, coef, heat):
    rows, total = own_0.shape
    return pl.pallas_call(
        first_body,
        in_specs=[IN_VMEM] * 5,
        out_specs=[IN_VMEM] * 4,
        out_shape=[jax.ShapeDtypeStruct((rows, total), F32)] * 2
        + [jax.ShapeDtypeStruct((rows - SIDE, total), BF16)] * 2,
        scratch_shapes=[pltpu.VMEM((2 * rows, total), BF16)],
        compiler_params=params(24),
        cost_estimate=pl.CostEstimate(
            flops=4 * rows * total * total, bytes_accessed=8 * MIB, transcendentals=0
        ),
        name="first_step",
    )(own_0, own_1, matrix, coef, heat)


def second_body(part_0, part_1, near_0, near_1, matrix, coef, heat, base_0, base_1, field, narrow):
    span, total = base_0.shape
    x_rate = coef[0:1, :]
    field[0] = part_0[...] + jnp.maximum(-x_rate, 0.0) * near_0[...].astype(F32)
    field[1] = part_1[...] + jnp.maximum(x_rate, 0.0) * near_1[...].astype(F32)
    for c in range(2):
        narrow[c * span : (c + 1) * span, :] = field[c, :span, :].astype(BF16)
    for first in range(0, total, TILE):
        at = pl.ds(first, TILE)
        x_rate = coef[0:1, at]
        scattered = scatter(matrix[at, :], narrow[...])
        mine_0, mine_1 = field[0, :, at], field[1, :, at]
        base_0[:, at] = local_terms(
            scattered[:span], mine_0, mine_1, jnp.maximum(x_rate, 0.0), coef[:, at], heat[:span, 0:1]
        )
        base_1[:, at] = local_terms(
            scattered[span:], mine_1, mine_0, jnp.maximum(-x_rate, 0.0), coef[:, at], heat[:span, 1:2]
        )


def second_step(part_0, part_1, near_0, near_1, matrix, coef, heat):
    rows, total = part_0.shape
    span = rows - SIDE
    return pl.pallas_call(
        second_body,
        in_specs=[IN_VMEM] * 7,
        out_specs=[IN_VMEM] * 2,
        out_shape=[jax.ShapeDtypeStruct((span, total), F32)] * 2,
        scratch_shapes=[pltpu.VMEM((2, rows, total), F32), pltpu.VMEM((2 * span, total), BF16)],
        compiler_params=params(24),
        cost_estimate=pl.CostEstimate(
            flops=4 * rows * total * total, bytes_accessed=8 * MIB, transcendentals=0
        ),
        name="second_step",
    )(part_0, part_1, near_0, near_1, matrix, coef, heat)


def finish_body(base_0, base_1, near_0, near_1, coef, result):
    groups, modes, cells = result.shape
    even = lax.axis_index("cell") % 2 == 0
    span = cells // 2
    unit = one_hot(iota((span, span), 0) == iota((span, span), 1))
    together = 4
    wide = together * modes
    for first in range(0, groups, together):
        lanes = pl.ds(first // together * wide, wide)
        x_rate = coef[0:1, lanes]
        for c, base, outer, rate in (
            (0, base_0, near_0, jnp.maximum(-x_rate, 0.0)),
            (1, base_1, near_1, jnp.maximum(x_rate, 0.0)),
        ):
            at = pl.ds(pl.multiple_of(jnp.where(even, 1 - c, c) * span, span), span)
            value = base[:, lanes] + rate * outer[:, lanes].astype(F32)
            turned = lax.dot_general(
                value.astype(BF16), unit, (((0,), (0,)), ((), ())), preferred_element_type=F32
            ).astype(BF16)
            for k in range(together):
                result[first + k, :, at] = turned[k * modes : (k + 1) * modes]


def finish(base_0, base_1, near_0, near_1, coef, groups):
    span, total = base_0.shape
    return pl.pallas_call(
        finish_body,
        out_shape=jax.ShapeDtypeStruct((groups, total // groups, 2 * span), BF16),
        compiler_params=params(32),
        cost_estimate=pl.CostEstimate(flops=10**7, bytes_accessed=3 * MIB, transcendentals=0),
        name="finish",
    )(base_0, base_1, near_0, near_1, coef)


def spread_body(result, out, wide, sent):
    groups, modes, cells = result.shape
    span, per = cells // 2, groups // PIECES
    row, lane = iota((2 * modes, 2 * modes), 0), iota((2 * modes, 2 * modes), 1)
    join = one_hot(row == jnp.where(lane < modes, 2 * lane, 2 * (lane - modes) + 1))
    copies = []
    for k in range(PIECES):
        for group in range(k * per, (k + 1) * per):
            both = jnp.concatenate([result[group, :, :span], result[group, :, span:]], axis=0)
            both = jnp.dot(join, both, preferred_element_type=F32)
            wide[:, :, pl.ds(group * span, span)] = both.reshape(modes, 2, span)
        at = pl.ds(k * per * span, per * span)
        copies.append(pltpu.make_async_copy(wide.at[:, :, at], out.at[:, :, at], sent.at[k]))
        copies[-1].start()
    for copy in copies:
        copy.wait()


def spread(result, cols):
    groups, modes, cells = result.shape
    shape = (modes, cols, groups * cells // cols)
    return pl.pallas_call(
        spread_body,
        in_specs=[IN_VMEM],
        out_specs=IN_HBM,
        out_shape=jax.ShapeDtypeStruct(shape, F32),
        scratch_shapes=[pltpu.VMEM(shape, F32), pltpu.SemaphoreType.DMA((PIECES,))],
        compiler_params=params(24),
        cost_estimate=pl.CostEstimate(flops=10**7, bytes_accessed=3 * MIB, transcendentals=0),
        name="spread",
    )(result)


def shards(initial, scatter_matrix, speed_x, speed_y, relaxation, emission, heater):
    modes, cols, length = initial.shape
    groups = lax.axis_size("mode")
    span = length // groups

    packed = pack(initial, (speed_x, speed_y, relaxation, emission), groups)
    received = lax.all_to_all(packed, "mode", 0, 0, tiled=True)
    own_0, own_1, coef, heat = unpack(received, heater)
    near_0, near_1 = swap(own_0, own_1)
    part_0, part_1, sent_0, sent_1 = first_step(own_0, own_1, scatter_matrix, coef, heat)
    far_0, far_1 = swap(sent_0, sent_1)
    base_0, base_1 = second_step(part_0, part_1, near_0, near_1, scatter_matrix, coef, heat)
    result = finish(base_0, base_1, far_0, far_1, coef, groups)
    result = lax.all_to_all(result, "mode", 0, 0, tiled=True)
    return spread(result, cols)


def solution(mesh):
    return jax.shard_map(
        shards,
        mesh=mesh,
        in_specs=(
            P("mode", "cell", None),
            P(),
            P("mode"),
            P("mode"),
            P("mode"),
            P("mode"),
            P("cell", None),
        ),
        out_specs=P("mode", "cell", None),
        check_vma=False,
    )
```

```python
import jax
import jax.numpy as jnp
from jax import lax
from jax.experimental import pallas as pl
from jax.experimental.pallas import tpu as pltpu
from jax.sharding import PartitionSpec as P

F32 = jnp.float32
BF16 = jnp.bfloat16
SIDE = 8
TILE = 256
MIB = 1024 * 1024
PIECES = 4


def swap(to_first, to_second):
    count = lax.axis_size("cell")
    first = [(i, i ^ 1) for i in range(count)]
    second = [(i, i + 1 if i % 2 else i - 1) for i in range(count)]
    inside = lambda pairs: [(i, j) for i, j in pairs if 0 <= j < count]
    return (
        lax.ppermute(to_first, "cell", inside(first)),
        lax.ppermute(to_second, "cell", inside(second)),
    )


IN_VMEM = pl.BlockSpec(memory_space=pltpu.VMEM)
IN_HBM = pl.BlockSpec(memory_space=pltpu.HBM)


def params(limit):
    return pltpu.CompilerParams(vmem_limit_bytes=limit * MIB)


def one_hot(mask):
    return jnp.where(mask, 1.0, 0.0).astype(BF16)


def iota(shape, axis):
    return lax.broadcasted_iota(jnp.int32, shape, axis)


def pack_body(rates, initial, packed):
    groups, height, cells = packed.shape
    modes, span = height - SIDE, cells // 2
    per = groups // PIECES
    wide = 2 * modes
    row, lane = iota((wide, wide), 0), iota((wide, wide), 1)
    apart = one_hot(lane == jnp.where(row < modes, 2 * row, 2 * (row - modes) + 1))
    row, lane = iota((per * span, groups * SIDE), 0), iota((per * span, groups * SIDE), 1)
    after = (lane // 2) % 2 == 0
    target = lane // SIDE * span + lane % 2 + jnp.where(after, span, -2) - row
    ends = jnp.zeros((wide, groups * SIDE), F32)
    for k in range(PIECES):
        first = k * per * span
        both = [
            initial[:, :, pl.ds(first + g * span, span)].reshape(wide, span).astype(BF16)
            for g in range(per)
        ]
        both = jnp.concatenate(both, axis=1)
        ends += jnp.dot(both, one_hot(target == first), preferred_element_type=F32)
        both = jnp.dot(apart, both, preferred_element_type=F32).astype(BF16)
        for g in range(per):
            at = slice(g * span, (g + 1) * span)
            packed[k * per + g, :modes, :] = jnp.concatenate([both[:modes, at], both[modes:, at]], axis=1)
    ends = jnp.dot(apart, ends.astype(BF16), preferred_element_type=F32)
    ends = jnp.concatenate(
        [ends[:modes], jnp.zeros((span - modes, groups * SIDE), F32),
         ends[modes:], jnp.zeros((span - modes, groups * SIDE), F32)], axis=0
    ).T
    middle = (iota((groups * SIDE, span), 0) % SIDE) // 2
    ends = jnp.where((middle == 1) | (middle == 2), ends[:, span:], ends[:, :span])
    sx, sy, relaxation, emission = (rates[k : k + 1, :] for k in range(4))
    inverse = 1.0 / (relaxation + jnp.abs(sx) + jnp.abs(sy))
    vectors = jnp.concatenate([sx * inverse, sy * inverse, inverse, emission * inverse], axis=0)
    high = vectors.astype(BF16).astype(F32)
    vectors = jnp.concatenate([high, vectors - high], axis=0)
    vectors = jnp.concatenate([vectors, jnp.zeros((SIDE, span - modes), F32)], axis=1)
    for group in range(groups):
        edge = ends[group * SIDE : (group + 1) * SIDE]
        packed[group, modes:, :] = jnp.concatenate([edge, vectors], axis=1).astype(BF16)


def pack(initial, rates, groups):
    modes, cols, length = initial.shape
    shape = (groups, modes + SIDE, cols * length // groups)
    return pl.pallas_call(
        pack_body,
        in_specs=[IN_VMEM] * 2,
        out_specs=IN_VMEM,
        out_shape=jax.ShapeDtypeStruct(shape, BF16),
        compiler_params=params(24),
        cost_estimate=pl.CostEstimate(flops=10**7, bytes_accessed=3 * MIB, transcendentals=0),
        name="pack",
    )(rates, initial)


def unpack_body(received, own_0, own_1, coef):
    groups, height, cells = received.shape
    modes, span = height - SIDE, cells // 2
    unit = one_hot(iota((span, span), 0) == iota((span, span), 1))
    even = lax.axis_index("cell") % 2 == 0
    together = 4
    wide = together * modes
    for first in range(0, groups, together):
        lanes = pl.ds(first // together * wide, wide)
        members = range(first, first + together)
        edge = jnp.concatenate([received[j, modes:, :modes] for j in members], axis=1).astype(F32)
        vector = jnp.concatenate(
            [received[j, modes:, span : span + modes] for j in members], axis=1
        ).astype(F32)
        vector = vector + pltpu.roll(vector, 4, 0)
        sign = jnp.where((iota((SIDE, wide), 0) == 0) & jnp.logical_not(even), -1.0, 1.0)
        coef[:, lanes] = vector * sign
        other = pltpu.roll(edge, 4, 0)
        for c, out in ((0, own_0), (1, own_1)):
            column = jnp.where(even, 1 - c, c)
            at = pl.ds(pl.multiple_of(column * span, span), span)
            block = jnp.concatenate([received[j, :modes, at] for j in members], axis=0)
            turned = lax.dot_general(
                unit, block, (((1,), (1,)), ((), ())), preferred_element_type=F32
            )
            ends = jnp.where(column == 0, edge, other)
            out[:, lanes] = jnp.concatenate([turned, ends], axis=0).astype(BF16)


def unpack(received):
    groups, height, cells = received.shape
    total, rows = groups * (height - SIDE), cells // 2 + SIDE
    return pl.pallas_call(
        unpack_body,
        in_specs=[IN_VMEM],
        out_specs=[IN_VMEM] * 3,
        out_shape=[jax.ShapeDtypeStruct((rows, total), BF16)] * 2
        + [jax.ShapeDtypeStruct((SIDE, total), F32)],
        compiler_params=params(24),
        cost_estimate=pl.CostEstimate(flops=10**7, bytes_accessed=3 * MIB, transcendentals=0),
        name="unpack",
    )(received)


def scatter(matrix, values):
    return lax.dot_general(
        values, matrix, (((1,), (1,)), ((), ())), preferred_element_type=F32
    )


def local_terms(scattered, mine, other, x_rate, coef, heat):
    rows, kept = mine.shape[0], scattered.shape[0]
    y_rate, inverse, emit = (coef[k : k + 1, :] for k in (1, 2, 3))
    return (
        scattered * inverse
        + heat * emit
        + jnp.maximum(y_rate, 0.0) * pltpu.roll(mine, 1, 0)[:kept]
        + jnp.maximum(-y_rate, 0.0) * pltpu.roll(mine, rows - 1, 0)[:kept]
        + x_rate * other[:kept]
    )


def first_body(own_0, own_1, matrix, coef, heater, part_0, part_1, sent_0, sent_1, heat, both):
    rows, total = own_0.shape
    span = rows - SIDE
    groups = heater.shape[1] // span
    me = lax.axis_index("mode")
    even = lax.axis_index("cell") % 2 == 0
    parts = []
    for k in (-1, 0, 1):
        there = me + k
        inside = ((there >= 0) & (there < groups)).astype(jnp.int32)
        at = pl.ds(pl.multiple_of(jnp.clip(there, 0, groups - 1) * span, span), span)
        parts.append(heater[:, at] * inside)
    near = jnp.concatenate(parts, axis=1).astype(F32)
    near = jnp.where(even, jnp.concatenate([near[1:], near[:1]], axis=0), near)
    near = jnp.concatenate([near, jnp.zeros((SIDE - 2, 3 * span), F32)], axis=0).astype(BF16)
    row, lane = iota((span + SIDE, 3 * span), 0), iota((span + SIDE, 3 * span), 1)
    pick = one_hot(lane == jnp.where(row < span + SIDE // 2, span + row, row - SIDE))
    heat[...] = lax.dot_general(pick, near, (((1,), (1,)), ((), ())), preferred_element_type=F32)
    both[:rows, :] = own_0[...].astype(F32).astype(BF16)
    both[rows:, :] = own_1[...].astype(F32).astype(BF16)
    for first in range(0, total, TILE):
        at = pl.ds(first, TILE)
        x_rate = coef[0:1, at]
        wide_0, wide_1 = own_0[:, at].astype(F32), own_1[:, at].astype(F32)
        scattered = scatter(matrix[at, :], both[...])
        value = local_terms(
            scattered[:rows], wide_0, wide_1, jnp.maximum(x_rate, 0.0), coef[:, at], heat[:, 0:1]
        )
        part_0[:, at] = value
        sent_0[:, at] = value[:span].astype(BF16)
        value = local_terms(
            scattered[rows:], wide_1, wide_0, jnp.maximum(-x_rate, 0.0), coef[:, at], heat[:, 1:2]
        )
        part_1[:, at] = value
        sent_1[:, at] = value[:span].astype(BF16)


def first_step(own_0, own_1, matrix, coef, heater):
    rows, total = own_0.shape
    return pl.pallas_call(
        first_body,
        in_specs=[IN_VMEM] * 5,
        out_specs=[IN_VMEM] * 5,
        out_shape=[jax.ShapeDtypeStruct((rows, total), F32)] * 2
        + [jax.ShapeDtypeStruct((rows - SIDE, total), BF16)] * 2
        + [jax.ShapeDtypeStruct((rows, SIDE), F32)],
        scratch_shapes=[pltpu.VMEM((2 * rows, total), BF16)],
        compiler_params=params(24),
        cost_estimate=pl.CostEstimate(
            flops=4 * rows * total * total, bytes_accessed=8 * MIB, transcendentals=0
        ),
        name="first_step",
    )(own_0, own_1, matrix, coef, heater)


def second_body(part_0, part_1, near_0, near_1, matrix, coef, heat, base_0, base_1, field, narrow):
    span, total = base_0.shape
    x_rate = coef[0:1, :]
    field[0] = part_0[...] + jnp.maximum(-x_rate, 0.0) * near_0[...].astype(F32)
    field[1] = part_1[...] + jnp.maximum(x_rate, 0.0) * near_1[...].astype(F32)
    for c in range(2):
        narrow[c * span : (c + 1) * span, :] = field[c, :span, :].astype(BF16)
    for first in range(0, total, TILE):
        at = pl.ds(first, TILE)
        x_rate = coef[0:1, at]
        scattered = scatter(matrix[at, :], narrow[...])
        mine_0, mine_1 = field[0, :, at], field[1, :, at]
        base_0[:, at] = local_terms(
            scattered[:span], mine_0, mine_1, jnp.maximum(x_rate, 0.0), coef[:, at], heat[:span, 0:1]
        )
        base_1[:, at] = local_terms(
            scattered[span:], mine_1, mine_0, jnp.maximum(-x_rate, 0.0), coef[:, at], heat[:span, 1:2]
        )


def second_step(part_0, part_1, near_0, near_1, matrix, coef, heat):
    rows, total = part_0.shape
    span = rows - SIDE
    return pl.pallas_call(
        second_body,
        in_specs=[IN_VMEM] * 7,
        out_specs=[IN_VMEM] * 2,
        out_shape=[jax.ShapeDtypeStruct((span, total), F32)] * 2,
        scratch_shapes=[pltpu.VMEM((2, rows, total), F32), pltpu.VMEM((2 * span, total), BF16)],
        compiler_params=params(24),
        cost_estimate=pl.CostEstimate(
            flops=4 * rows * total * total, bytes_accessed=8 * MIB, transcendentals=0
        ),
        name="second_step",
    )(part_0, part_1, near_0, near_1, matrix, coef, heat)


def finish_body(base_0, base_1, near_0, near_1, coef, result):
    groups, modes, cells = result.shape
    even = lax.axis_index("cell") % 2 == 0
    span = cells // 2
    unit = one_hot(iota((span, span), 0) == iota((span, span), 1))
    together = 4
    wide = together * modes
    for first in range(0, groups, together):
        lanes = pl.ds(first // together * wide, wide)
        x_rate = coef[0:1, lanes]
        for c, base, outer, rate in (
            (0, base_0, near_0, jnp.maximum(-x_rate, 0.0)),
            (1, base_1, near_1, jnp.maximum(x_rate, 0.0)),
        ):
            at = pl.ds(pl.multiple_of(jnp.where(even, 1 - c, c) * span, span), span)
            value = base[:, lanes] + rate * outer[:, lanes].astype(F32)
            turned = lax.dot_general(
                value.astype(BF16), unit, (((0,), (0,)), ((), ())), preferred_element_type=F32
            ).astype(BF16)
            for k in range(together):
                result[first + k, :, at] = turned[k * modes : (k + 1) * modes]


def finish(base_0, base_1, near_0, near_1, coef, groups):
    span, total = base_0.shape
    return pl.pallas_call(
        finish_body,
        out_shape=jax.ShapeDtypeStruct((groups, total // groups, 2 * span), BF16),
        compiler_params=params(32),
        cost_estimate=pl.CostEstimate(flops=10**7, bytes_accessed=3 * MIB, transcendentals=0),
        name="finish",
    )(base_0, base_1, near_0, near_1, coef)


def spread_body(result, out, wide, sent):
    groups, modes, cells = result.shape
    span, per = cells // 2, groups // PIECES
    row, lane = iota((2 * modes, 2 * modes), 0), iota((2 * modes, 2 * modes), 1)
    join = one_hot(row == jnp.where(lane < modes, 2 * lane, 2 * (lane - modes) + 1))
    copies = []
    for k in range(PIECES):
        for group in range(k * per, (k + 1) * per):
            both = jnp.concatenate([result[group, :, :span], result[group, :, span:]], axis=0)
            both = jnp.dot(join, both, preferred_element_type=F32)
            wide[:, :, pl.ds(group * span, span)] = both.reshape(modes, 2, span)
        at = pl.ds(k * per * span, per * span)
        copies.append(pltpu.make_async_copy(wide.at[:, :, at], out.at[:, :, at], sent.at[k]))
        copies[-1].start()
    for copy in copies:
        copy.wait()


def spread(result, cols):
    groups, modes, cells = result.shape
    shape = (modes, cols, groups * cells // cols)
    return pl.pallas_call(
        spread_body,
        in_specs=[IN_VMEM],
        out_specs=IN_HBM,
        out_shape=jax.ShapeDtypeStruct(shape, F32),
        scratch_shapes=[pltpu.VMEM(shape, F32), pltpu.SemaphoreType.DMA((PIECES,))],
        compiler_params=params(24),
        cost_estimate=pl.CostEstimate(flops=10**7, bytes_accessed=3 * MIB, transcendentals=0),
        name="spread",
    )(result)


def shards(initial, scatter_matrix, speed_x, speed_y, relaxation, emission, heater):
    modes, cols, length = initial.shape
    groups = lax.axis_size("mode")
    span = length // groups

    packed = pack(initial, jnp.stack([speed_x, speed_y, relaxation, emission]), groups)
    received = lax.all_to_all(packed, "mode", 0, 0, tiled=True)
    own_0, own_1, coef = unpack(received)
    near_0, near_1 = swap(own_0, own_1)
    part_0, part_1, sent_0, sent_1, heat = first_step(own_0, own_1, scatter_matrix, coef, heater)
    far_0, far_1 = swap(sent_0, sent_1)
    base_0, base_1 = second_step(part_0, part_1, near_0, near_1, scatter_matrix, coef, heat)
    result = finish(base_0, base_1, far_0, far_1, coef, groups)
    result = lax.all_to_all(result, "mode", 0, 0, tiled=True)
    return spread(result, cols)


def solution(mesh):
    return jax.shard_map(
        shards,
        mesh=mesh,
        in_specs=(
            P("mode", "cell", None),
            P(),
            P("mode"),
            P("mode"),
            P("mode"),
            P("mode"),
            P("cell", None),
        ),
        out_specs=P("mode", "cell", None),
        check_vma=False,
    )
```

```python
import jax
import jax.numpy as jnp
from jax import lax
from jax.experimental import pallas as pl
from jax.experimental.pallas import tpu as pltpu
from jax.sharding import PartitionSpec as P

F32 = jnp.float32
BF16 = jnp.bfloat16
SIDE = 8
TILE = 256
MIB = 1024 * 1024
PIECES = 8


def swap(to_first, to_second):
    count = lax.axis_size("cell")
    first = [(i, i ^ 1) for i in range(count)]
    second = [(i, i + 1 if i % 2 else i - 1) for i in range(count)]
    inside = lambda pairs: [(i, j) for i, j in pairs if 0 <= j < count]
    return (
        lax.ppermute(to_first, "cell", inside(first)),
        lax.ppermute(to_second, "cell", inside(second)),
    )


IN_VMEM = pl.BlockSpec(memory_space=pltpu.VMEM)
IN_HBM = pl.BlockSpec(memory_space=pltpu.HBM)


def params(limit):
    return pltpu.CompilerParams(vmem_limit_bytes=limit * MIB)


def one_hot(mask):
    return jnp.where(mask, 1.0, 0.0).astype(BF16)


def iota(shape, axis):
    return lax.broadcasted_iota(jnp.int32, shape, axis)


def pack_body(rates, initial, packed):
    groups, height, cells = packed.shape
    modes, span = height - SIDE, cells // 2
    per = groups // PIECES
    wide = 2 * modes
    row, lane = iota((wide, wide), 0), iota((wide, wide), 1)
    apart = one_hot(lane == jnp.where(row < modes, 2 * row, 2 * (row - modes) + 1))
    row, lane = iota((per * span, groups * SIDE), 0), iota((per * span, groups * SIDE), 1)
    after = (lane // 2) % 2 == 0
    target = lane // SIDE * span + lane % 2 + jnp.where(after, span, -2) - row
    ends = jnp.zeros((wide, groups * SIDE), F32)
    for k in range(PIECES):
        first = k * per * span
        both = [
            initial[:, :, pl.ds(first + g * span, span)].reshape(wide, span).astype(BF16)
            for g in range(per)
        ]
        both = jnp.concatenate(both, axis=1)
        ends += jnp.dot(both, one_hot(target == first), preferred_element_type=F32)
        both = jnp.dot(apart, both, preferred_element_type=F32).astype(BF16)
        for g in range(per):
            at = slice(g * span, (g + 1) * span)
            packed[k * per + g, :modes, :] = jnp.concatenate([both[:modes, at], both[modes:, at]], axis=1)
    ends = jnp.dot(apart, ends.astype(BF16), preferred_element_type=F32)
    ends = jnp.concatenate(
        [ends[:modes], jnp.zeros((span - modes, groups * SIDE), F32),
         ends[modes:], jnp.zeros((span - modes, groups * SIDE), F32)], axis=0
    ).T
    middle = (iota((groups * SIDE, span), 0) % SIDE) // 2
    ends = jnp.where((middle == 1) | (middle == 2), ends[:, span:], ends[:, :span])
    sx, sy, relaxation, emission = (rates[k : k + 1, :] for k in range(4))
    inverse = 1.0 / (relaxation + jnp.abs(sx) + jnp.abs(sy))
    vectors = jnp.concatenate([sx * inverse, sy * inverse, inverse, emission * inverse], axis=0)
    high = vectors.astype(BF16).astype(F32)
    vectors = jnp.concatenate([high, vectors - high], axis=0)
    vectors = jnp.concatenate([vectors, jnp.zeros((SIDE, span - modes), F32)], axis=1)
    for group in range(groups):
        edge = ends[group * SIDE : (group + 1) * SIDE]
        packed[group, modes:, :] = jnp.concatenate([edge, vectors], axis=1).astype(BF16)


def pack(initial, rates, groups):
    modes, cols, length = initial.shape
    shape = (groups, modes + SIDE, cols * length // groups)
    return pl.pallas_call(
        pack_body,
        in_specs=[IN_VMEM] * 2,
        out_specs=IN_VMEM,
        out_shape=jax.ShapeDtypeStruct(shape, BF16),
        compiler_params=params(24),
        cost_estimate=pl.CostEstimate(flops=10**7, bytes_accessed=3 * MIB, transcendentals=0),
        name="pack",
    )(rates, initial)


def unpack_body(received, own_0, own_1):
    groups, height, cells = received.shape
    modes, span = height - SIDE, cells // 2
    unit = one_hot(iota((span, span), 0) == iota((span, span), 1))
    even = lax.axis_index("cell") % 2 == 0
    together = 8
    wide = together * modes
    for first in range(0, groups, together):
        lanes = pl.ds(first // together * wide, wide)
        members = range(first, first + together)
        edge = jnp.concatenate([received[j, modes:, :modes] for j in members], axis=1).astype(F32)
        other = pltpu.roll(edge, 4, 0)
        for c, out in ((0, own_0), (1, own_1)):
            column = jnp.where(even, 1 - c, c)
            at = pl.ds(pl.multiple_of(column * span, span), span)
            block = jnp.concatenate([received[j, :modes, at] for j in members], axis=0)
            turned = lax.dot_general(
                unit, block, (((1,), (1,)), ((), ())), preferred_element_type=F32
            )
            ends = jnp.where(column == 0, edge, other)
            out[:, lanes] = jnp.concatenate([turned, ends], axis=0).astype(BF16)


def unpack(received):
    groups, height, cells = received.shape
    total, rows = groups * (height - SIDE), cells // 2 + SIDE
    return pl.pallas_call(
        unpack_body,
        in_specs=[IN_VMEM],
        out_specs=[IN_VMEM] * 2,
        out_shape=[jax.ShapeDtypeStruct((rows, total), BF16)] * 2,
        compiler_params=params(24),
        cost_estimate=pl.CostEstimate(flops=10**7, bytes_accessed=3 * MIB, transcendentals=0),
        name="unpack",
    )(received)


def scatter(matrix, values):
    return lax.dot_general(
        values, matrix, (((1,), (1,)), ((), ())), preferred_element_type=F32
    )


def local_terms(scattered, mine, other, x_rate, coef, heat):
    rows, kept = mine.shape[0], scattered.shape[0]
    y_rate, inverse, emit = (coef[k : k + 1, :] for k in (1, 2, 3))
    return (
        scattered * inverse
        + heat * emit
        + jnp.maximum(y_rate, 0.0) * pltpu.roll(mine, 1, 0)[:kept]
        + jnp.maximum(-y_rate, 0.0) * pltpu.roll(mine, rows - 1, 0)[:kept]
        + x_rate * other[:kept]
    )


def first_body(own_0, own_1, matrix, received, heater, part_0, part_1, sent_0, sent_1, heat, coef, both):
    rows, total = own_0.shape
    span = rows - SIDE
    groups, height, _ = received.shape
    modes = height - SIDE
    together = 4
    wide = together * modes
    even = lax.axis_index("cell") % 2 == 0
    for first in range(0, groups, together):
        lanes = pl.ds(first // together * wide, wide)
        members = range(first, first + together)
        vector = jnp.concatenate(
            [received[j, modes:, span : span + modes] for j in members], axis=1
        ).astype(F32)
        vector = vector + pltpu.roll(vector, 4, 0)
        sign = jnp.where((iota((SIDE, wide), 0) == 0) & jnp.logical_not(even), -1.0, 1.0)
        coef[:, lanes] = vector * sign
    me = lax.axis_index("mode")
    parts = []
    for k in (-1, 0, 1):
        there = me + k
        inside = ((there >= 0) & (there < groups)).astype(jnp.int32)
        at = pl.ds(pl.multiple_of(jnp.clip(there, 0, groups - 1) * span, span), span)
        parts.append(heater[:, at] * inside)
    near = jnp.concatenate(parts, axis=1).astype(F32)
    near = jnp.where(even, jnp.concatenate([near[1:], near[:1]], axis=0), near)
    near = jnp.concatenate([near, jnp.zeros((SIDE - 2, 3 * span), F32)], axis=0).astype(BF16)
    row, lane = iota((span + SIDE, 3 * span), 0), iota((span + SIDE, 3 * span), 1)
    pick = one_hot(lane == jnp.where(row < span + SIDE // 2, span + row, row - SIDE))
    heat[...] = lax.dot_general(pick, near, (((1,), (1,)), ((), ())), preferred_element_type=F32)
    both[:rows, :] = own_0[...].astype(F32).astype(BF16)
    both[rows:, :] = own_1[...].astype(F32).astype(BF16)
    for first in range(0, total, TILE):
        at = pl.ds(first, TILE)
        x_rate = coef[0:1, at]
        wide_0, wide_1 = own_0[:, at].astype(F32), own_1[:, at].astype(F32)
        scattered = scatter(matrix[at, :], both[...])
        value = local_terms(
            scattered[:rows], wide_0, wide_1, jnp.maximum(x_rate, 0.0), coef[:, at], heat[:, 0:1]
        )
        part_0[:, at] = value
        sent_0[:, at] = value[:span].astype(BF16)
        value = local_terms(
            scattered[rows:], wide_1, wide_0, jnp.maximum(-x_rate, 0.0), coef[:, at], heat[:, 1:2]
        )
        part_1[:, at] = value
        sent_1[:, at] = value[:span].astype(BF16)


def first_step(own_0, own_1, matrix, received, heater):
    rows, total = own_0.shape
    return pl.pallas_call(
        first_body,
        in_specs=[IN_VMEM] * 5,
        out_specs=[IN_VMEM] * 6,
        out_shape=[jax.ShapeDtypeStruct((rows, total), F32)] * 2
        + [jax.ShapeDtypeStruct((rows - SIDE, total), BF16)] * 2
        + [jax.ShapeDtypeStruct((rows, SIDE), F32), jax.ShapeDtypeStruct((SIDE, total), F32)],
        scratch_shapes=[pltpu.VMEM((2 * rows, total), BF16)],
        compiler_params=params(24),
        cost_estimate=pl.CostEstimate(
            flops=4 * rows * total * total, bytes_accessed=8 * MIB, transcendentals=0
        ),
        name="first_step",
    )(own_0, own_1, matrix, received, heater)


def second_body(part_0, part_1, near_0, near_1, matrix, coef, heat, base_0, base_1, field, narrow):
    span, total = base_0.shape
    x_rate = coef[0:1, :]
    field[0] = part_0[...] + jnp.maximum(-x_rate, 0.0) * near_0[...].astype(F32)
    field[1] = part_1[...] + jnp.maximum(x_rate, 0.0) * near_1[...].astype(F32)
    for c in range(2):
        narrow[c * span : (c + 1) * span, :] = field[c, :span, :].astype(BF16)
    for first in range(0, total, TILE):
        at = pl.ds(first, TILE)
        x_rate = coef[0:1, at]
        scattered = scatter(matrix[at, :], narrow[...])
        mine_0, mine_1 = field[0, :, at], field[1, :, at]
        base_0[:, at] = local_terms(
            scattered[:span], mine_0, mine_1, jnp.maximum(x_rate, 0.0), coef[:, at], heat[:span, 0:1]
        )
        base_1[:, at] = local_terms(
            scattered[span:], mine_1, mine_0, jnp.maximum(-x_rate, 0.0), coef[:, at], heat[:span, 1:2]
        )


def second_step(part_0, part_1, near_0, near_1, matrix, coef, heat):
    rows, total = part_0.shape
    span = rows - SIDE
    return pl.pallas_call(
        second_body,
        in_specs=[IN_VMEM] * 7,
        out_specs=[IN_VMEM] * 2,
        out_shape=[jax.ShapeDtypeStruct((span, total), F32)] * 2,
        scratch_shapes=[pltpu.VMEM((2, rows, total), F32), pltpu.VMEM((2 * span, total), BF16)],
        compiler_params=params(24),
        cost_estimate=pl.CostEstimate(
            flops=4 * rows * total * total, bytes_accessed=8 * MIB, transcendentals=0
        ),
        name="second_step",
    )(part_0, part_1, near_0, near_1, matrix, coef, heat)


def finish_body(base_0, base_1, near_0, near_1, coef, result):
    groups, modes, cells = result.shape
    even = lax.axis_index("cell") % 2 == 0
    span = cells // 2
    unit = one_hot(iota((span, span), 0) == iota((span, span), 1))
    together = 4
    wide = together * modes
    for first in range(0, groups, together):
        lanes = pl.ds(first // together * wide, wide)
        x_rate = coef[0:1, lanes]
        for c, base, outer, rate in (
            (0, base_0, near_0, jnp.maximum(-x_rate, 0.0)),
            (1, base_1, near_1, jnp.maximum(x_rate, 0.0)),
        ):
            at = pl.ds(pl.multiple_of(jnp.where(even, 1 - c, c) * span, span), span)
            value = base[:, lanes] + rate * outer[:, lanes].astype(F32)
            turned = lax.dot_general(
                value.astype(BF16), unit, (((0,), (0,)), ((), ())), preferred_element_type=F32
            ).astype(BF16)
            for k in range(together):
                result[first + k, :, at] = turned[k * modes : (k + 1) * modes]


def finish(base_0, base_1, near_0, near_1, coef, groups):
    span, total = base_0.shape
    return pl.pallas_call(
        finish_body,
        out_shape=jax.ShapeDtypeStruct((groups, total // groups, 2 * span), BF16),
        compiler_params=params(32),
        cost_estimate=pl.CostEstimate(flops=10**7, bytes_accessed=3 * MIB, transcendentals=0),
        name="finish",
    )(base_0, base_1, near_0, near_1, coef)


def spread_body(result, out, wide, sent):
    groups, modes, cells = result.shape
    span, per = cells // 2, groups // PIECES
    row, lane = iota((2 * modes, 2 * modes), 0), iota((2 * modes, 2 * modes), 1)
    join = one_hot(row == jnp.where(lane < modes, 2 * lane, 2 * (lane - modes) + 1))
    copies = []
    for k in range(PIECES):
        for group in range(k * per, (k + 1) * per):
            both = jnp.concatenate([result[group, :, :span], result[group, :, span:]], axis=0)
            both = jnp.dot(join, both, preferred_element_type=F32)
            wide[:, :, pl.ds(group * span, span)] = both.reshape(modes, 2, span)
        at = pl.ds(k * per * span, per * span)
        copies.append(pltpu.make_async_copy(wide.at[:, :, at], out.at[:, :, at], sent.at[k]))
        copies[-1].start()
    for copy in copies:
        copy.wait()


def spread(result, cols):
    groups, modes, cells = result.shape
    shape = (modes, cols, groups * cells // cols)
    return pl.pallas_call(
        spread_body,
        in_specs=[IN_VMEM],
        out_specs=IN_HBM,
        out_shape=jax.ShapeDtypeStruct(shape, F32),
        scratch_shapes=[pltpu.VMEM(shape, F32), pltpu.SemaphoreType.DMA((PIECES,))],
        compiler_params=params(24),
        cost_estimate=pl.CostEstimate(flops=10**7, bytes_accessed=3 * MIB, transcendentals=0),
        name="spread",
    )(result)


def shards(initial, scatter_matrix, speed_x, speed_y, relaxation, emission, heater):
    modes, cols, length = initial.shape
    groups = lax.axis_size("mode")
    span = length // groups

    packed = pack(initial, jnp.stack([speed_x, speed_y, relaxation, emission]), groups)
    received = lax.all_to_all(packed, "mode", 0, 0, tiled=True)
    own_0, own_1 = unpack(received)
    near_0, near_1 = swap(own_0, own_1)
    part_0, part_1, sent_0, sent_1, heat, coef = first_step(
        own_0, own_1, scatter_matrix, received, heater
    )
    far_0, far_1 = swap(sent_0, sent_1)
    base_0, base_1 = second_step(part_0, part_1, near_0, near_1, scatter_matrix, coef, heat)
    result = finish(base_0, base_1, far_0, far_1, coef, groups)
    result = lax.all_to_all(result, "mode", 0, 0, tiled=True)
    return spread(result, cols)


def solution(mesh):
    return jax.shard_map(
        shards,
        mesh=mesh,
        in_specs=(
            P("mode", "cell", None),
            P(),
            P("mode"),
            P("mode"),
            P("mode"),
            P("mode"),
            P("cell", None),
        ),
        out_specs=P("mode", "cell", None),
        check_vma=False,
    )
```

```python
import jax
import jax.numpy as jnp
from jax import lax
from jax.experimental import pallas as pl
from jax.experimental.pallas import tpu as pltpu
from jax.sharding import PartitionSpec as P

F32 = jnp.float32
BF16 = jnp.bfloat16
SIDE = 8
TILE = 256
MIB = 1024 * 1024
PIECES = 8


def swap(to_first, to_second):
    count = lax.axis_size("cell")
    first = [(i, i ^ 1) for i in range(count)]
    second = [(i, i + 1 if i % 2 else i - 1) for i in range(count)]
    inside = lambda pairs: [(i, j) for i, j in pairs if 0 <= j < count]
    return (
        lax.ppermute(to_first, "cell", inside(first)),
        lax.ppermute(to_second, "cell", inside(second)),
    )


IN_VMEM = pl.BlockSpec(memory_space=pltpu.VMEM)
IN_HBM = pl.BlockSpec(memory_space=pltpu.HBM)


def params(limit):
    return pltpu.CompilerParams(vmem_limit_bytes=limit * MIB)


def one_hot(mask):
    return jnp.where(mask, 1.0, 0.0).astype(BF16)


def iota(shape, axis):
    return lax.broadcasted_iota(jnp.int32, shape, axis)


def pack_body(rates, initial, packed):
    groups, height, cells = packed.shape
    modes, span = height - SIDE, cells // 2
    per = groups // PIECES
    wide = 2 * modes
    row, lane = iota((wide, wide), 0), iota((wide, wide), 1)
    apart = one_hot(lane == jnp.where(row < modes, 2 * row, 2 * (row - modes) + 1))
    row, lane = iota((per * span, groups * SIDE), 0), iota((per * span, groups * SIDE), 1)
    after = (lane // 2) % 2 == 0
    target = lane // SIDE * span + lane % 2 + jnp.where(after, span, -2) - row
    ends = jnp.zeros((wide, groups * SIDE), F32)
    for k in range(PIECES):
        first = k * per * span
        both = [
            initial[:, :, pl.ds(first + g * span, span)].reshape(wide, span).astype(BF16)
            for g in range(per)
        ]
        both = jnp.concatenate(both, axis=1)
        ends += jnp.dot(both, one_hot(target == first), preferred_element_type=F32)
        both = jnp.dot(apart, both, preferred_element_type=F32).astype(BF16)
        for g in range(per):
            at = slice(g * span, (g + 1) * span)
            packed[k * per + g, :modes, :] = jnp.concatenate([both[:modes, at], both[modes:, at]], axis=1)
    ends = jnp.dot(apart, ends.astype(BF16), preferred_element_type=F32)
    ends = jnp.concatenate(
        [ends[:modes], jnp.zeros((span - modes, groups * SIDE), F32),
         ends[modes:], jnp.zeros((span - modes, groups * SIDE), F32)], axis=0
    ).T
    middle = (iota((groups * SIDE, span), 0) % SIDE) // 2
    ends = jnp.where((middle == 1) | (middle == 2), ends[:, span:], ends[:, :span])
    sx, sy, relaxation, emission = (rates[k : k + 1, :] for k in range(4))
    inverse = 1.0 / (relaxation + jnp.abs(sx) + jnp.abs(sy))
    vectors = jnp.concatenate([sx * inverse, sy * inverse, inverse, emission * inverse], axis=0)
    high = vectors.astype(BF16).astype(F32)
    vectors = jnp.concatenate([high, vectors - high], axis=0)
    vectors = jnp.concatenate([vectors, jnp.zeros((SIDE, span - modes), F32)], axis=1)
    for group in range(groups):
        edge = ends[group * SIDE : (group + 1) * SIDE]
        packed[group, modes:, :] = jnp.concatenate([edge, vectors], axis=1).astype(BF16)


def pack(initial, rates, groups):
    modes, cols, length = initial.shape
    shape = (groups, modes + SIDE, cols * length // groups)
    return pl.pallas_call(
        pack_body,
        in_specs=[IN_VMEM] * 2,
        out_specs=IN_VMEM,
        out_shape=jax.ShapeDtypeStruct(shape, BF16),
        compiler_params=params(24),
        cost_estimate=pl.CostEstimate(flops=10**7, bytes_accessed=3 * MIB, transcendentals=0),
        name="pack",
    )(rates, initial)


def unpack_body(received, own_0, own_1):
    groups, height, cells = received.shape
    modes, span = height - SIDE, cells // 2
    unit = one_hot(iota((span, span), 0) == iota((span, span), 1))
    even = lax.axis_index("cell") % 2 == 0
    together = 8
    wide = together * modes
    for first in range(0, groups, together):
        lanes = pl.ds(first // together * wide, wide)
        members = range(first, first + together)
        edge = jnp.concatenate([received[j, modes:, :modes] for j in members], axis=1).astype(F32)
        other = pltpu.roll(edge, 4, 0)
        for c, out in ((0, own_0), (1, own_1)):
            column = jnp.where(even, 1 - c, c)
            at = pl.ds(pl.multiple_of(column * span, span), span)
            block = jnp.concatenate([received[j, :modes, at] for j in members], axis=0)
            turned = lax.dot_general(
                unit, block, (((1,), (1,)), ((), ())), preferred_element_type=F32
            )
            ends = jnp.where(column == 0, edge, other)
            out[:, lanes] = jnp.concatenate([turned, ends], axis=0).astype(BF16)


def unpack(received):
    groups, height, cells = received.shape
    total, rows = groups * (height - SIDE), cells // 2 + SIDE
    return pl.pallas_call(
        unpack_body,
        in_specs=[IN_VMEM],
        out_specs=[IN_VMEM] * 2,
        out_shape=[jax.ShapeDtypeStruct((rows, total), BF16)] * 2,
        compiler_params=params(24),
        cost_estimate=pl.CostEstimate(flops=10**7, bytes_accessed=3 * MIB, transcendentals=0),
        name="unpack",
    )(received)


def scatter(matrix, values):
    return lax.dot_general(
        values, matrix, (((1,), (1,)), ((), ())), preferred_element_type=F32
    )


def local_terms(scattered, mine, other, x_rate, coef, heat):
    rows, kept = mine.shape[0], scattered.shape[0]
    y_rate, inverse, emit = (coef[k : k + 1, :] for k in (1, 2, 3))
    return (
        scattered * inverse
        + heat * emit
        + jnp.maximum(y_rate, 0.0) * pltpu.roll(mine, 1, 0)[:kept]
        + jnp.maximum(-y_rate, 0.0) * pltpu.roll(mine, rows - 1, 0)[:kept]
        + x_rate * other[:kept]
    )


def first_body(own_0, own_1, matrix, received, heater, part_0, part_1, sent_0, sent_1, heat, coef, both):
    rows, total = own_0.shape
    span = rows - SIDE
    groups, height, _ = received.shape
    modes = height - SIDE
    together = 4
    wide = together * modes
    even = lax.axis_index("cell") % 2 == 0
    for first in range(0, groups, together):
        lanes = pl.ds(first // together * wide, wide)
        members = range(first, first + together)
        vector = jnp.concatenate(
            [received[j, modes:, span : span + modes] for j in members], axis=1
        ).astype(F32)
        vector = vector + pltpu.roll(vector, 4, 0)
        sign = jnp.where((iota((SIDE, wide), 0) == 0) & jnp.logical_not(even), -1.0, 1.0)
        coef[:, lanes] = vector * sign
    me = lax.axis_index("mode")
    parts = []
    for k in (-1, 0, 1):
        there = me + k
        inside = ((there >= 0) & (there < groups)).astype(jnp.int32)
        at = pl.ds(pl.multiple_of(jnp.clip(there, 0, groups - 1) * span, span), span)
        parts.append(heater[:, at] * inside)
    near = jnp.concatenate(parts, axis=1).astype(F32)
    near = jnp.where(even, jnp.concatenate([near[1:], near[:1]], axis=0), near)
    near = jnp.concatenate([near, jnp.zeros((SIDE - 2, 3 * span), F32)], axis=0).astype(BF16)
    row, lane = iota((span + SIDE, 3 * span), 0), iota((span + SIDE, 3 * span), 1)
    pick = one_hot(lane == jnp.where(row < span + SIDE // 2, span + row, row - SIDE))
    heat[...] = lax.dot_general(pick, near, (((1,), (1,)), ((), ())), preferred_element_type=F32)
    both[:rows, :] = own_0[...]
    both[rows:, :] = own_1[...]
    for first in range(0, total, TILE):
        at = pl.ds(first, TILE)
        x_rate = coef[0:1, at]
        wide_0, wide_1 = own_0[:, at].astype(F32), own_1[:, at].astype(F32)
        scattered = scatter(matrix[at, :], both[...])
        value = local_terms(
            scattered[:rows], wide_0, wide_1, jnp.maximum(x_rate, 0.0), coef[:, at], heat[:, 0:1]
        )
        part_0[:, at] = value
        sent_0[:, at] = value[:span].astype(BF16)
        value = local_terms(
            scattered[rows:], wide_1, wide_0, jnp.maximum(-x_rate, 0.0), coef[:, at], heat[:, 1:2]
        )
        part_1[:, at] = value
        sent_1[:, at] = value[:span].astype(BF16)


def first_step(own_0, own_1, matrix, received, heater):
    rows, total = own_0.shape
    return pl.pallas_call(
        first_body,
        in_specs=[IN_VMEM] * 5,
        out_specs=[IN_VMEM] * 6,
        out_shape=[jax.ShapeDtypeStruct((rows, total), F32)] * 2
        + [jax.ShapeDtypeStruct((rows - SIDE, total), BF16)] * 2
        + [jax.ShapeDtypeStruct((rows, SIDE), F32), jax.ShapeDtypeStruct((SIDE, total), F32)],
        scratch_shapes=[pltpu.VMEM((2 * rows, total), BF16)],
        compiler_params=params(24),
        cost_estimate=pl.CostEstimate(
            flops=4 * rows * total * total, bytes_accessed=8 * MIB, transcendentals=0
        ),
        name="first_step",
    )(own_0, own_1, matrix, received, heater)


def second_body(part_0, part_1, near_0, near_1, matrix, coef, heat, base_0, base_1, field, narrow):
    span, total = base_0.shape
    x_rate = coef[0:1, :]
    field[0] = part_0[...] + jnp.maximum(-x_rate, 0.0) * near_0[...].astype(F32)
    field[1] = part_1[...] + jnp.maximum(x_rate, 0.0) * near_1[...].astype(F32)
    for c in range(2):
        narrow[c * span : (c + 1) * span, :] = field[c, :span, :].astype(BF16)
    for first in range(0, total, TILE):
        at = pl.ds(first, TILE)
        x_rate = coef[0:1, at]
        scattered = scatter(matrix[at, :], narrow[...])
        mine_0, mine_1 = field[0, :, at], field[1, :, at]
        base_0[:, at] = local_terms(
            scattered[:span], mine_0, mine_1, jnp.maximum(x_rate, 0.0), coef[:, at], heat[:span, 0:1]
        )
        base_1[:, at] = local_terms(
            scattered[span:], mine_1, mine_0, jnp.maximum(-x_rate, 0.0), coef[:, at], heat[:span, 1:2]
        )


def second_step(part_0, part_1, near_0, near_1, matrix, coef, heat):
    rows, total = part_0.shape
    span = rows - SIDE
    return pl.pallas_call(
        second_body,
        in_specs=[IN_VMEM] * 7,
        out_specs=[IN_VMEM] * 2,
        out_shape=[jax.ShapeDtypeStruct((span, total), F32)] * 2,
        scratch_shapes=[pltpu.VMEM((2, rows, total), F32), pltpu.VMEM((2 * span, total), BF16)],
        compiler_params=params(24),
        cost_estimate=pl.CostEstimate(
            flops=4 * rows * total * total, bytes_accessed=8 * MIB, transcendentals=0
        ),
        name="second_step",
    )(part_0, part_1, near_0, near_1, matrix, coef, heat)


def finish_body(base_0, base_1, near_0, near_1, coef, result):
    groups, modes, cells = result.shape
    even = lax.axis_index("cell") % 2 == 0
    span = cells // 2
    unit = one_hot(iota((span, span), 0) == iota((span, span), 1))
    together = 4
    wide = together * modes
    for first in range(0, groups, together):
        lanes = pl.ds(first // together * wide, wide)
        x_rate = coef[0:1, lanes]
        for c, base, outer, rate in (
            (0, base_0, near_0, jnp.maximum(-x_rate, 0.0)),
            (1, base_1, near_1, jnp.maximum(x_rate, 0.0)),
        ):
            at = pl.ds(pl.multiple_of(jnp.where(even, 1 - c, c) * span, span), span)
            value = base[:, lanes] + rate * outer[:, lanes].astype(F32)
            turned = lax.dot_general(
                value.astype(BF16), unit, (((0,), (0,)), ((), ())), preferred_element_type=F32
            ).astype(BF16)
            for k in range(together):
                result[first + k, :, at] = turned[k * modes : (k + 1) * modes]


def finish(base_0, base_1, near_0, near_1, coef, groups):
    span, total = base_0.shape
    return pl.pallas_call(
        finish_body,
        out_shape=jax.ShapeDtypeStruct((groups, total // groups, 2 * span), BF16),
        compiler_params=params(32),
        cost_estimate=pl.CostEstimate(flops=10**7, bytes_accessed=3 * MIB, transcendentals=0),
        name="finish",
    )(base_0, base_1, near_0, near_1, coef)


def spread_body(result, out, wide, sent):
    groups, modes, cells = result.shape
    span, per = cells // 2, groups // PIECES
    row, lane = iota((2 * modes, 2 * modes), 0), iota((2 * modes, 2 * modes), 1)
    join = one_hot(row == jnp.where(lane < modes, 2 * lane, 2 * (lane - modes) + 1))
    copies = []
    for k in range(PIECES):
        at = pl.ds(k * per * span, per * span)
        both = [
            jnp.concatenate([result[group, :, :span], result[group, :, span:]], axis=0)
            for group in range(k * per, (k + 1) * per)
        ]
        both = jnp.dot(join, jnp.concatenate(both, axis=1), preferred_element_type=F32)
        wide[:, :, at] = both.reshape(modes, 2, per * span)
        copies.append(pltpu.make_async_copy(wide.at[:, :, at], out.at[:, :, at], sent.at[k]))
        copies[-1].start()
    for copy in copies:
        copy.wait()


def spread(result, cols):
    groups, modes, cells = result.shape
    shape = (modes, cols, groups * cells // cols)
    return pl.pallas_call(
        spread_body,
        in_specs=[IN_VMEM],
        out_specs=IN_HBM,
        out_shape=jax.ShapeDtypeStruct(shape, F32),
        scratch_shapes=[pltpu.VMEM(shape, F32), pltpu.SemaphoreType.DMA((PIECES,))],
        compiler_params=params(24),
        cost_estimate=pl.CostEstimate(flops=10**7, bytes_accessed=3 * MIB, transcendentals=0),
        name="spread",
    )(result)


def shards(initial, scatter_matrix, speed_x, speed_y, relaxation, emission, heater):
    modes, cols, length = initial.shape
    groups = lax.axis_size("mode")
    span = length // groups

    packed = pack(initial, jnp.stack([speed_x, speed_y, relaxation, emission]), groups)
    received = lax.all_to_all(packed, "mode", 0, 0, tiled=True)
    own_0, own_1 = unpack(received)
    near_0, near_1 = swap(own_0, own_1)
    part_0, part_1, sent_0, sent_1, heat, coef = first_step(
        own_0, own_1, scatter_matrix, received, heater
    )
    far_0, far_1 = swap(sent_0, sent_1)
    base_0, base_1 = second_step(part_0, part_1, near_0, near_1, scatter_matrix, coef, heat)
    result = finish(base_0, base_1, far_0, far_1, coef, groups)
    result = lax.all_to_all(result, "mode", 0, 0, tiled=True)
    return spread(result, cols)


def solution(mesh):
    return jax.shard_map(
        shards,
        mesh=mesh,
        in_specs=(
            P("mode", "cell", None),
            P(),
            P("mode"),
            P("mode"),
            P("mode"),
            P("mode"),
            P("cell", None),
        ),
        out_specs=P("mode", "cell", None),
        check_vma=False,
    )
```
